512 devices in a mesh: dp: 32 (over z, y_hi), tensor: 16 (over y_lo, x, core).
Axes of the slice: x: 4, y: 8 (y_hi: 4, y_lo: 2; y = y_hi * 2 + y_lo), z: 8, core: 2. Of those that a mesh axis runs over, the one named last changes fastest.
Arguments:
- activations: bfloat16 [256, 128, 8192], P('dp', None, 'tensor'), may hold values from -6 to 6
- cotangents: bfloat16 [256, 128, 8192], P('dp', None, 'tensor'), may hold values from -6 to 6
- lengths: int32 [256], P('dp'), may hold values from 32 to 128
- adapter_down_matrix: bfloat16 [8192, 8], P('tensor'), may hold values from -0.0625 to 0.0625
- adapter_up_matrix: bfloat16 [8, 8192], P(None, 'tensor'), may hold values from -0.0625 to 0.0625
- projection: bfloat16 [131072, 4096], P('tensor', 'dp'), may hold values from -0.015625 to 0.015625
- validation_gradient_rows: bfloat16 [256, 4096], P(None, 'dp'), may hold values from -6 to 6
Outputs:
- scores: float32 [256, 256], P('tensor')
The draws below stay inside these ranges and needn't reach their ends.
All inputs are finite; a program needn't handle non-finite values.
Results may differ from the reference program's by a relative error of at most 0.0041.
Values may be sent and summed in bfloat16 or wider, within the bound.
A program may use at most 64 MiB of HBM per device.

```python
import math
import jax
import jax.numpy as jnp
from jax import lax

MODEL_WIDTH = 8192
ADAPTER_RANK = 8
K = 4096
VAL = 256
SEQ = 128
TRAIN = 256
G = 131072


def set_ends(result, key, least, largest):
    index_at = [jax.random.randint(jax.random.fold_in(key, axis), (), 0, length) for axis, length in enumerate(result.shape)]
    widest = result.shape.index(max(result.shape))
    neighbour = index_at[:widest] + [(index_at[widest] + 1) % result.shape[widest]] + index_at[widest + 1:]
    return result.at[tuple(index_at)].set(least).at[tuple(neighbour)].set(largest)


def shard_levels(rng, dims, split, low, top_value):
    loudness, own = 1.0, jax.random.fold_in(rng, 6)
    for position, blocks in split:
        heights = jnp.exp(jax.random.uniform(jax.random.fold_in(own, position), (blocks,), jnp.float32, low / len(split), top_value / len(split)))
        loudness = loudness * jnp.repeat(heights, dims[position] // blocks).reshape([-1 if axis == position else 1 for axis in range(len(dims))])
    return loudness


def noise(own_key, dims, deviation, bound, cuts=(), held_as=jnp.bfloat16):
    loudness = shard_levels(own_key, dims, cuts, -0.22, 0.18) if cuts else 1.0
    drawn = jax.random.normal(own_key, dims, jnp.float32) * deviation * loudness
    return jnp.minimum(jnp.maximum(drawn, -bound), bound).astype(held_as)


def setup_inputs(seed: int = 0) -> dict:
    seeds = jax.random.split(jax.random.key(seed), 8)
    activations = noise(seeds[0], (TRAIN, SEQ, MODEL_WIDTH), 1.0, 6.0, ((0, 32), (2, 16)))
    cotangents = noise(seeds[1], (TRAIN, SEQ, MODEL_WIDTH), 1.0, 6.0, ((0, 32), (2, 16)))
    lengths = set_ends(jax.random.randint(seeds[2], (TRAIN,), SEQ // 4, SEQ + 1), jax.random.fold_in(seeds[2], 1), SEQ // 4, SEQ).astype(jnp.int32)
    adapter_down_matrix = noise(seeds[3], (MODEL_WIDTH, ADAPTER_RANK), MODEL_WIDTH ** -0.5, 0.0625, ((0, 16),))
    adapter_up_matrix = noise(seeds[4], (ADAPTER_RANK, MODEL_WIDTH), MODEL_WIDTH ** -0.5, 0.0625, ((1, 16),))
    projection = noise(seeds[5], (G, K), G ** -0.5, 0.015625, ((0, 16), (1, 32)))
    validation_gradient_rows = noise(seeds[6], (VAL, K), 1.0, 6.0, ((1, 32),))
    return {"activations": activations, "cotangents": cotangents, "lengths": lengths, "adapter_down_matrix": adapter_down_matrix, "adapter_up_matrix": adapter_up_matrix, "projection": projection, "validation_gradient_rows": validation_gradient_rows}


adapter_scale = 2.0
epsilon = 1e-06

def reference(activations, cotangents, lengths, adapter_down_matrix, adapter_up_matrix, projection, validation_gradient_rows):
    token_positions = jnp.arange(SEQ, dtype=jnp.int32)
    weight_values = (token_positions[None, :] < lengths[:, None]).astype(jnp.float32) * adapter_scale

    def one_example(operands):
        input_batch, output_batch, weight_row = operands
        down_hidden_state = jnp.dot(input_batch, adapter_down_matrix, preferred_element_type=jnp.float32)
        up_hidden_state = jnp.dot(output_batch, adapter_up_matrix.T, preferred_element_type=jnp.float32)
        left_factor = (weight_row[:, None] * up_hidden_state).astype(jnp.bfloat16)
        right_factor = (weight_row[:, None] * down_hidden_state).astype(jnp.bfloat16)
        grad_down = jnp.dot(input_batch.T, left_factor, preferred_element_type=jnp.float32)
        grad_up = jnp.dot(output_batch.T, right_factor, preferred_element_type=jnp.float32)
        return jnp.concatenate([grad_down, grad_up], axis=1).reshape(-1).astype(jnp.bfloat16)
    gradients = lax.map(one_example, (activations, cotangents, weight_values))
    projected = jnp.dot(gradients, projection, preferred_element_type=jnp.float32)
    target = validation_gradient_rows.astype(jnp.float32)
    train_sq = lax.optimization_barrier(jnp.sum(projected * projected, axis=1))
    target_sq = lax.optimization_barrier(jnp.sum(target * target, axis=1))
    inner = jnp.dot(projected, target.T, precision=lax.Precision.HIGHEST, preferred_element_type=jnp.float32)
    factor = math.sqrt(K)
    return factor * inner * lax.rsqrt(train_sq + epsilon)[:, None] * lax.rsqrt(target_sq + epsilon)[None, :]
```

```python
import heapq
import math

import jax
import jax.numpy as jnp
from jax import lax
from jax.experimental import pallas as pl
from jax.experimental.pallas import tpu as pltpu
from jax.sharding import PartitionSpec as P

MESH = pl.DeviceIdType.MESH
K = 4096
SCALE = 2.0
EPS = 1e-06
NZ, NY, NT = 8, 4, 16
NA = 5
NB = 8 - NA
WA, WB = NA * 512, NB * 512
HALF = (NA * 512 // 256) * 128
PLUS = {0: 4, 1: 3, 2: 4, 3: 3}
F32, BF16 = jnp.float32, jnp.bfloat16


def hops(r, way):
    return PLUS[r] if way == "+" else 7 - PLUS[r]


def follow(tag, halves):
    kind = tag[0]
    ta, tb = NA * 0.328, NB * 0.328

    def along_z(r):
        return [("z+", ("Az", r, "+", 1), ta), ("z-", ("Az", r, "-", 1), ta)]

    def along_y(o):
        return [("y+", ("By", "+", o), 2 * tb), ("y-", ("By", "-", o), 2 * tb)]

    if kind == "own":
        first = [("y+", ("Ay", 3), 2 * ta), ("y-", ("Ay", 1), 2 * ta)]
        first += [("z+", ("Bz", "+", 1), tb), ("z-", ("Bz", "-", 1), tb)]
        return first + along_z(0) + along_y(0)
    if kind == "Ay":
        if tag[1] == 3:
            return [("y+", ("Ay", "2a"), ta)] + along_z(3)
        if tag[1] == 1:
            return [("y-", ("Ay", "2b"), ta)] + along_z(1)
        halves.append(tag)
        return along_z(2) if len(halves) == 2 else []
    if kind == "Az":
        _, r, way, h = tag
        return [("z" + way, ("Az", r, way, h + 1), ta)] if h < hops(r, way) else []
    if kind == "Bz":
        _, way, h = tag
        on = [("z" + way, ("Bz", way, h + 1), tb)] if h < (4 if way == "+" else 3) else []
        return on + along_y(-h if way == "+" else h)
    if kind == "By":
        _, way, o = tag
        return [("y" + way, ("Bo", way, o), 2 * tb)] if (o % 2 == 0) == (way == "+") else []
    return []


def plan():
    free = dict.fromkeys(("z+", "z-", "y+", "y-"), 0.0)
    heap, order, halves, count = [(0.0, 0, ("own",))], [], [], 0
    while heap:
        now, _, tag = heapq.heappop(heap)
        sends = follow(tag, halves)
        order.append((tag, [(link, new) for link, new, _ in sends]))
        for link, new, length in sends:
            count += 1
            free[link] = max(now, free[link]) + length
            heapq.heappush(heap, (free[link] + 1.5, count, new))
    return order


ORDER = plan()
TAGS = [tag for tag, _ in ORDER[1:]]
TAGS += [(k, r) for k in ("h", "f", "p") for r in range(1, NT)]
TAGS += [(k, r) for k in ("y1", "y2", "ty") for r in range(1, NY)]
TAGS += [(k, r) for k in ("z1", "tz") for r in range(1, NZ)]
INDEX = {tag: i for i, tag in enumerate(TAGS)}


def kernel(
    act_in, cot_in, lengths, down, up, proj_in, target, out,
    act, cot, proj, pc, ga, gb, hid, hrecv, facs, parta, partb, sbuf, precv,
    tq, tqy, tqz, y1s, y1r, z1r, fin, lsem, ssem, rsem,
):
    dp, me = lax.axis_index("dp"), lax.axis_index("tensor")
    z, y = lax.div(dp, NY), lax.rem(dp, NY)

    def at_z(o):
        return lax.rem(z + (o % NZ), NZ)

    def at_y(o):
        return lax.rem(y + (o % NY), NY)

    def at_t(o):
        return lax.rem(me + (o % NT), NT)

    def dev(zz, yy):
        return (zz * NY + yy, me)

    def copy(tag, src, dst, device):
        i = INDEX[tag]
        return pltpu.make_async_remote_copy(
            src_ref=src, dst_ref=dst, send_sem=ssem.at[i], recv_sem=rsem.at[i],
            device_id=device, device_id_type=MESH,
        )

    sent = []

    def send(tag, src, dst, device):
        c = copy(tag, src, dst, device)
        c.start()
        sent.append(c)

    def wait(tag, ref):
        copy(tag, ref, ref, dev(at_z(1), y)).wait_recv()

    loads = [
        pltpu.make_async_copy(a, b, lsem.at[i])
        for i, (a, b) in enumerate(((act_in, act), (cot_in, cot), (proj_in, proj)))
    ]
    for c in loads:
        c.start()

    barrier = pltpu.get_barrier_semaphore()
    partners = [(dp, at_t(r)) for r in range(1, NT)]
    partners += [dev(at_z(o), y) for o in range(1, NZ)] + [dev(z, at_y(o)) for o in range(1, NY)]
    for p in partners:
        pl.semaphore_signal(barrier, inc=1, device_id=p, device_id_type=MESH)

    nt = (((1,), (1,)), ((), ()))
    loads[0].wait()
    for e in range(8):
        hid[8 + e] = lax.dot_general(down[...], act[e], nt, preferred_element_type=F32)
    loads[1].wait()
    for e in range(8):
        hid[e] = lax.dot_general(up[...], cot[e], nt, preferred_element_type=F32)
    pl.semaphore_wait(barrier, len(partners))
    for r in range(1, NT):
        p = at_t(r)
        send(("h", r), hid.at[p], hrecv.at[me], (dp, p))
    hrecv[me] = hid[me]

    rows = target[...].astype(F32)
    ones = jnp.ones((8, 128), F32)
    norms = lax.dot_general(
        ones, rows * rows, nt, precision=lax.Precision.HIGHEST, preferred_element_type=F32
    )
    which = lax.broadcasted_iota(jnp.int32, (8, 128), 0)
    tq[...] = jnp.where(which == 0, norms[:, :128], norms[:, 128:])
    for r in range(1, NY):
        send(("ty", r), tq, tqy.at[y], dev(z, at_y(r)))
    tqy[y] = tq[...]

    q = lax.broadcasted_iota(jnp.int32, (256, 256), 0)
    c = lax.broadcasted_iota(jnp.int32, (256, 256), 1)
    swap = jnp.where(c == lax.rem(q, 16) * 16 + lax.div(q, 16), 1.0, 0.0).astype(BF16)

    def turn(b, carry):
        block = proj[pl.ds(pl.multiple_of(b * 256, 256), 256), :]
        moved = jnp.dot(swap, block, preferred_element_type=F32).astype(BF16)
        for j in range(16):
            at = pl.ds(pl.multiple_of(b * 16 + (j % 8) * 512, 16), 16)
            pc[at, (j // 8) * 128 : (j // 8) * 128 + 128] = moved[j * 16 : j * 16 + 16]
        return carry

    loads[2].wait()
    lax.fori_loop(0, 16, turn, 0)

    for r in range(1, NT):
        wait(("h", r), hrecv.at[at_t(-r)])
    total = hrecv[0]
    for t in range(1, NT):
        total = total + hrecv[t]
    token = lax.broadcasted_iota(jnp.int32, (8, 128), 1)
    facs[me] = jnp.where(token < lengths[lax.rem(me, 8)], SCALE, 0.0) * total
    for r in range(1, NT):
        send(("f", r), facs.at[me], facs.at[me], (dp, at_t(r)))

    for r in range(1, NY):
        wait(("ty", r), tqy.at[at_y(-r)])
    tqz[z] = (tqy[0] + tqy[1]) + (tqy[2] + tqy[3])
    for r in range(1, NZ):
        send(("tz", r), tqz.at[z], tqz.at[z], dev(at_z(r), y))
    lax.fori_loop(16, 32, turn, 0)

    for r in range(1, NT):
        wait(("f", r), facs.at[at_t(-r)])
    own = lax.broadcasted_iota(jnp.int32, (8, 8, 128), 1)
    grads = []
    for a, data in ((0, act), (1, cot)):
        parts = []
        for e in range(8):
            spread = jnp.broadcast_to(facs[a * 8 + e][:, None, :], (8, 8, 128))
            parts.append(jnp.where(own == e, spread, 0.0).reshape(64, 128).astype(BF16))
        left = jnp.concatenate(parts, axis=1)
        grads.append(jnp.dot(left, data[...].reshape(1024, 512), preferred_element_type=F32))
    for j in range(8):
        tile = jnp.concatenate([g[j * 8 : j * 8 + 8] for g in grads], axis=0).astype(BF16)
        if j < NA:
            ga[dp, :, j * 512 : j * 512 + 512] = tile
        else:
            gb[y * NZ + z, :, (j - NA) * 512 : (j - NA) * 512 + 512] = tile

    def slot(tag):
        kind = tag[0]
        if kind == "Ay":
            if tag[1] in (1, 3):
                return ga.at[z * NY + at_y(tag[1])]
            lanes = pl.ds(0, HALF) if tag[1] == "2a" else pl.ds(HALF, WA - HALF)
            return ga.at[z * NY + at_y(2), :, lanes]
        if kind == "Az":
            _, r, way, h = tag
            return ga.at[at_z(-h if way == "+" else h) * NY + at_y(r)]
        if kind == "Bz":
            _, way, h = tag
            return gb.at[y * NZ + at_z(-h if way == "+" else h)]
        _, way, o = tag
        r = 2 if kind == "Bo" else (-1 if way == "+" else 1)
        return gb.at[at_y(r) * NZ + at_z(o)]

    def source(link, new):
        kind = new[0]
        s = 1 if link[1] == "+" else -1
        if kind == "Ay":
            if new[1] in (1, 3):
                return ga.at[dp]
            lanes = pl.ds(0, HALF) if new[1] == "2a" else pl.ds(HALF, WA - HALF)
            return ga.at[z * NY + at_y(-s), :, lanes]
        if kind == "Az":
            _, r, _, h = new
            return ga.at[at_z(-s * (h - 1)) * NY + at_y(r)]
        if kind == "Bz":
            return gb.at[y * NZ + at_z(-s * (new[2] - 1))]
        o = new[2]
        return gb.at[(y if kind == "By" else at_y(-s)) * NZ + at_z(o)]

    def fold(found):
        found = found.reshape(-1, 2, 8, 256)
        return found[:, 0, :, :128] + found[:, 1, :, 128:]

    def product_a(o):
        first = at_z(o) * NY
        block = ga[pl.ds(first, NY)].reshape(NY * 16, WA)
        parta[pl.ds(first, NY)] = fold(jnp.dot(block, pc[:WA, :], preferred_element_type=F32))

    def product_b(r):
        first = at_y(r) * NZ
        block = gb[pl.ds(first, NZ)].reshape(NZ * 16, WB)
        partb[pl.ds(first, NZ)] = fold(jnp.dot(block, pc[WA:, :], preferred_element_type=F32))

    need_a = {o: 4 for o in range(NZ)}
    need_b = {r: 8 for r in range(NY)}
    for tag, sends in ORDER:
        if tag != ("own",):
            wait(tag, slot(tag))
        for link, new in sends:
            step = 1 if link[1] == "+" else -1
            to = dev(at_z(step), y) if link[0] == "z" else dev(z, at_y(step))
            ref = source(link, new)
            send(new, ref, ref, to)
        kind = tag[0]
        if kind == "own":
            need_a[0] -= 1
            need_b[0] -= 1
        elif kind == "Ay":
            need_a[0] -= 1 if tag[1] in (1, 3) else 0.5
            if need_a[0] == 0:
                product_a(0)
        elif kind == "Az":
            o = (-tag[3] if tag[2] == "+" else tag[3]) % NZ
            need_a[o] -= 1
            if need_a[o] == 0:
                product_a(o)
        else:
            r = 0 if kind == "Bz" else 2 if kind == "Bo" else 3 if tag[1] == "+" else 1
            need_b[r] -= 1
            if need_b[r] == 0:
                product_b(r)
    assert not any(need_a.values()) and not any(need_b.values())

    for p in range(NT):
        pair = []
        for d in (2 * p, 2 * p + 1):
            pair.append(parta[d] + partb[(d % NY) * NZ + d // NY])
        sbuf[p] = jnp.concatenate(pair, axis=0)
    for r in range(1, NT):
        p = at_t(r)
        send(("p", r), sbuf.at[p], precv.at[me], (dp, p))
    precv[me] = sbuf[me]
    for r in range(1, NT):
        wait(("p", r), precv.at[at_t(-r)])
    projected = precv[0]
    for t in range(1, NT):
        projected = projected + precv[t]

    inner = lax.dot_general(
        projected, rows, nt, precision=lax.Precision.HIGHEST, preferred_element_type=F32
    )
    square = jnp.broadcast_to(jnp.sum(projected * projected, axis=1, keepdims=True), (16, 128))
    for i in range(NY):
        up_rows, lanes = slice((i // 2) * 8, (i // 2) * 8 + 8), slice((i % 2) * 128, (i % 2) * 128 + 128)
        y1s[i, 0] = inner[up_rows, lanes]
        y1s[i, 1] = square[up_rows, :]
    for r in range(1, NY):
        send(("y1", r), y1s.at[at_y(r)], y1r.at[y], dev(z, at_y(r)))
    y1r[y] = y1s[y]
    for r in range(1, NY):
        wait(("y1", r), y1r.at[at_y(-r)])
    z1r[z] = (y1r[0] + y1r[1]) + (y1r[2] + y1r[3])
    for r in range(1, NZ):
        send(("z1", r), z1r.at[z], z1r.at[z], dev(at_z(r), y))
    for r in range(1, NZ):
        wait(("tz", r), tqz.at[at_z(-r)])
    norm = tqz[0]
    for t in range(1, NZ):
        norm = norm + tqz[t]
    norm = jnp.where(lax.rem(y, 2) == 0, norm[0:1], norm[1:2])
    for r in range(1, NZ):
        wait(("z1", r), z1r.at[at_z(-r)])
    both = z1r[0]
    for t in range(1, NZ):
        both = both + z1r[t]
    fin[y] = math.sqrt(K) * both[0] * lax.rsqrt(both[1] + EPS) * lax.rsqrt(norm + EPS)
    for r in range(1, NY):
        send(("y2", r), fin.at[y], fin.at[y], dev(z, at_y(r)))
    for r in range(1, NY):
        wait(("y2", r), fin.at[at_y(-r)])
    for i in range(NY):
        out[(i // 2) * 8 : (i // 2) * 8 + 8, (i % 2) * 128 : (i % 2) * 128 + 128] = fin[i]
    for c in sent:
        c.wait_send()


def body(activations, cotangents, lengths, down, up, projection, target):
    vmem, hbm = pl.BlockSpec(memory_space=pltpu.VMEM), pl.BlockSpec(memory_space=pl.ANY)
    smem = pl.BlockSpec(memory_space=pltpu.SMEM)
    return pl.pallas_call(
        kernel,
        out_shape=jax.ShapeDtypeStruct((16, 256), F32),
        in_specs=[hbm, hbm, smem, vmem, vmem, hbm, vmem],
        out_specs=vmem,
        scratch_shapes=[
            pltpu.VMEM((8, 128, 512), BF16),
            pltpu.VMEM((8, 128, 512), BF16),
            pltpu.VMEM((8192, 128), BF16),
            pltpu.VMEM((4096, 256), BF16),
            pltpu.VMEM((32, 16, WA), BF16),
            pltpu.VMEM((32, 16, WB), BF16),
            pltpu.VMEM((16, 8, 128), F32),
            pltpu.VMEM((16, 8, 128), F32),
            pltpu.VMEM((16, 8, 128), F32),
            pltpu.VMEM((32, 8, 128), F32),
            pltpu.VMEM((32, 8, 128), F32),
            pltpu.VMEM((16, 16, 128), F32),
            pltpu.VMEM((16, 16, 128), F32),
            pltpu.VMEM((8, 128), F32),
            pltpu.VMEM((4, 8, 128), F32),
            pltpu.VMEM((8, 8, 128), F32),
            pltpu.VMEM((4, 2, 8, 128), F32),
            pltpu.VMEM((4, 2, 8, 128), F32),
            pltpu.VMEM((8, 2, 8, 128), F32),
            pltpu.VMEM((4, 8, 128), F32),
            pltpu.SemaphoreType.DMA((3,)),
            pltpu.SemaphoreType.DMA((len(TAGS),)),
            pltpu.SemaphoreType.DMA((len(TAGS),)),
        ],
        compiler_params=pltpu.CompilerParams(
            collective_id=0, has_side_effects=True, vmem_limit_bytes=40 * 1024 * 1024
        ),
    )(activations, cotangents, lengths, down.T, up, projection, target)


def solution(mesh):
    placed = (
        P("dp", None, "tensor"),
        P("dp", None, "tensor"),
        P("dp"),
        P("tensor", None),
        P(None, "tensor"),
        P("tensor", "dp"),
        P(None, "dp"),
    )
    return jax.shard_map(
        body, mesh=mesh, in_specs=placed, out_specs=P("tensor", None), check_vma=False
    )
```

```python
import heapq
import math

import jax
import jax.numpy as jnp
from jax import lax
from jax.experimental import pallas as pl
from jax.experimental.pallas import tpu as pltpu
from jax.sharding import PartitionSpec as P

MESH = pl.DeviceIdType.MESH
K = 4096
SCALE = 2.0
EPS = 1e-06
NZ, NY, NT = 8, 4, 16
W = 1024
F32, BF16 = jnp.float32, jnp.bfloat16


def onward(o, r):
    if o in (-1, 1):
        return [(3 * o, "z+" if o < 0 else "z-")]
    if o in (-2, 2) and (o < 0) == (r % 2 == 0):
        return [(4, "z+" if o < 0 else "z-")]
    return []


def follow(tag):
    kind = tag[0]
    if kind == "own":
        sends = [("y" + w, ("Ay", c, 3 if w == "+" else 1), 2) for c in "so" for w in "+-"]
        for o, links in ((1, 1), (2, 2)):
            sends += [("z+", ("Bz", -o), links), ("z-", ("Bz", o), links)]
        for o, links in ((1, 1), (2, 2)):
            sends += [("z+", ("Az", 0, -o), links), ("z-", ("Az", 0, o), links)]
        return sends + [("y+", ("By", "+", 0), 2), ("y-", ("By", "-", 0), 2)]
    if kind == "Ay":
        _, c, r = tag
        o = 2 if c == "s" else 1
        sends = [("z+", ("Az", r, -o), o), ("z-", ("Az", r, o), o)]
        if (c, r) in (("s", 3), ("o", 1)):
            sends = [("y+" if c == "s" else "y-", ("Ay", c, 2), 2)] + sends
        return sends
    if kind == "Az":
        return [(link, ("Az", tag[1], o), 2) for o, link in onward(tag[2], tag[1])]
    if kind == "Bz":
        on = [(link, ("Bz", o), 2) for o, link in onward(tag[1], 0)]
        return on + [("y+", ("By", "+", tag[1]), 2), ("y-", ("By", "-", tag[1]), 2)]
    if kind == "By" and (tag[2] % 2 == 0) == (tag[1] == "+"):
        return [("y" + tag[1], ("Bo", tag[1], tag[2]), 2)]
    return []


def plan():
    free = dict.fromkeys(("z+", "z-", "y+", "y-"), 0.0)
    heap, order, count = [(0.0, 0, ("own",))], [], 0
    while heap:
        now, _, tag = heapq.heappop(heap)
        sends = follow(tag)
        order.append((now, tag, [(link, new) for link, new, _ in sends]))
        for link, new, links in sends:
            count += 1
            free[link] = max(now, free[link]) + links * 0.655
            heapq.heappush(heap, (free[link] + 2.2 + 0.6 * links, count, new))
    return order


ORDER = [(tag, sends) for _, tag, sends in plan()]
TAGS = [tag for tag, _ in ORDER[1:]]
TAGS += [(k, r) for k in ("h", "f", "p") for r in range(1, NT)]
TAGS += [(k, r) for k in ("y1", "y2", "ty") for r in range(1, NY)]
TAGS += [(k, r) for k in ("z1", "tz") for r in range(1, NZ)]
TAGS += [("pu",), ("pd",)] + [("ra", o) for o in range(NZ)] + [("rb", r) for r in range(NY)]
INDEX = {tag: i for i, tag in enumerate(TAGS)}


def kernel(
    act_in, cot_in, lengths_in, down_in, up_in, proj_in, target_in, out,
    act, cot, lengths, down, up, proj, target, pc, neighbours, own_blocks, other, ga, gb, hid, hrecv, facs, pa, pb,
    sbuf, precv,
    tq, tqy, tqz, y1s, y1r, z1r, fin, lsem, ssem, rsem,
):
    dp, me = lax.axis_index("dp"), lax.axis_index("tensor")
    z, y = lax.div(dp, NY), lax.rem(dp, NY)
    parity = lax.rem(z, 2)

    def at_z(o):
        return lax.rem(z + (o % NZ), NZ)

    def at_y(o):
        return lax.rem(y + (o % NY), NY)

    def at_t(o):
        return lax.rem(me + (o % NT), NT)

    def dev(zz, yy):
        return (zz * NY + yy, me)

    def copy(tag, src, dst, device):
        i = INDEX[tag]
        return pltpu.make_async_remote_copy(
            src_ref=src, dst_ref=dst, send_sem=ssem.at[i], recv_sem=rsem.at[i],
            device_id=device, device_id_type=MESH,
        )

    sent = []

    def send(tag, src, dst, device):
        c = copy(tag, src, dst, device)
        c.start()
        sent.append(c)

    def wait(tag, ref):
        copy(tag, ref, ref, dev(at_z(1), y)).wait_recv()

    ends = (
        (down_in, down), (act_in, act), (up_in, up), (cot_in, cot),
        (target_in, target), (lengths_in, lengths), (proj_in, proj),
    )
    loads = [pltpu.make_async_copy(a, b, lsem.at[i]) for i, (a, b) in enumerate(ends)]
    for c in loads:
        c.start()

    barrier = pltpu.get_barrier_semaphore()
    partners = [(dp, at_t(r)) for r in range(1, NT)]
    partners += [dev(at_z(o), y) for o in range(1, NZ)] + [dev(z, at_y(o)) for o in range(1, NY)]
    for p in partners:
        pl.semaphore_signal(barrier, inc=1, device_id=p, device_id_type=MESH)

    nt = (((1,), (1,)), ((), ()))
    loads[0].wait()
    loads[1].wait()
    for e in range(8):
        hid[8 + e] = lax.dot_general(down[...], act[e], nt, preferred_element_type=F32)
    loads[2].wait()
    loads[3].wait()
    for e in range(8):
        hid[e] = lax.dot_general(up[...], cot[e], nt, preferred_element_type=F32)
    pl.semaphore_wait(barrier, len(partners))
    loads[6].wait()
    theirs = pl.multiple_of((1 - parity) * 4096, 4096)
    for r in range(1, NT):
        p = at_t(r)
        send(("h", r), hid.at[p], hrecv.at[me], (dp, p))
    send(("pu",), proj.at[pl.ds(theirs, 2048)], neighbours.at[0], dev(at_z(-1), y))
    send(("pd",), proj.at[pl.ds(theirs + 2048, 2048)], neighbours.at[1], dev(at_z(1), y))
    hrecv[me] = hid[me]

    loads[4].wait()
    rows = target[...].astype(F32)
    ones = jnp.ones((8, 128), F32)
    norms = lax.dot_general(
        ones, rows * rows, nt, precision=lax.Precision.HIGHEST, preferred_element_type=F32
    )
    which = lax.broadcasted_iota(jnp.int32, (8, 128), 0)
    tq[...] = jnp.where(which == 0, norms[:, :128], norms[:, 128:])
    for r in range(1, NY):
        send(("ty", r), tq, tqy.at[y], dev(z, at_y(r)))
    tqy[y] = tq[...]

    q = lax.broadcasted_iota(jnp.int32, (256, 256), 0)
    c = lax.broadcasted_iota(jnp.int32, (256, 256), 1)
    swap = jnp.where(c == lax.rem(q, 16) * 16 + lax.div(q, 16), 1.0, 0.0).astype(BF16)

    def turn(source, first, to):
        def step(b, carry):
            block = source[pl.ds(pl.multiple_of(first + b * 256, 256), 256), :]
            moved = jnp.dot(swap, block, preferred_element_type=F32).astype(BF16)
            for j in range(16):
                at = pl.ds(pl.multiple_of(b * 16 + (j % 8) * 128, 16), 16)
                to[at, (j // 8) * 128 : (j // 8) * 128 + 128] = moved[j * 16 : j * 16 + 16]
            return carry

        lax.fori_loop(0, 8, step, 0, unroll=True)

    mine = pl.multiple_of(parity * 4096, 4096)
    turn(proj, mine, pc.at[0])
    turn(proj, mine + 2048, pc.at[1])

    for r in range(1, NT):
        wait(("h", r), hrecv.at[at_t(-r)])
    total = hrecv[0]
    for t in range(1, NT):
        total = total + hrecv[t]
    loads[5].wait()
    token = lax.broadcasted_iota(jnp.int32, (8, 128), 1)
    facs[me] = jnp.where(token < lengths[lax.rem(me, 8)], SCALE, 0.0) * total
    for r in range(1, NT):
        send(("f", r), facs.at[me], facs.at[me], (dp, at_t(r)))

    for r in range(1, NY):
        wait(("ty", r), tqy.at[at_y(-r)])
    tqz[z] = (tqy[0] + tqy[1]) + (tqy[2] + tqy[3])
    for r in range(1, NZ):
        send(("tz", r), tqz.at[z], tqz.at[z], dev(at_z(r), y))

    for r in range(1, NT):
        wait(("f", r), facs.at[at_t(-r)])
    own = lax.broadcasted_iota(jnp.int32, (8, 8, 128), 1)
    grads = []
    for a, data in ((0, act), (1, cot)):
        parts = []
        for e in range(8):
            spread = jnp.broadcast_to(facs[a * 8 + e][:, None, :], (8, 8, 128))
            parts.append(jnp.where(own == e, spread, 0.0).reshape(64, 128).astype(BF16))
        left = jnp.concatenate(parts, axis=1)
        grads.append(jnp.dot(left, data[...].reshape(1024, 512), preferred_element_type=F32))
    for j in range(8):
        tile = jnp.concatenate([g[j * 8 : j * 8 + 8] for g in grads], axis=0).astype(BF16)
        for i in range(4):
            own_blocks[i, :, j * 128 : j * 128 + 128] = tile[:, i * 128 : i * 128 + 128]
    same, not_same = 2 * parity, 2 - 2 * parity
    ga[dp] = own_blocks[same]
    gb[y * NZ + z] = own_blocks[same + 1]

    def slot_a(o, r):
        return ga.at[at_z(o) * NY + at_y(r)]

    def slot_b(o, r):
        return gb.at[at_y(r) * NZ + at_z(o)]

    def slot(tag):
        kind = tag[0]
        if kind == "Ay":
            return slot_a(0, tag[2]) if tag[1] == "s" else other.at[tag[2] - 1]
        if kind == "Az":
            return slot_a(tag[2], tag[1])
        if kind == "Bz":
            return slot_b(tag[1], 0)
        return slot_b(tag[2], 2 if kind == "Bo" else 3 if tag[1] == "+" else 1)

    def ends_of(link, new):
        kind = new[0]
        s = 1 if link[1] == "+" else -1
        if kind == "Ay":
            _, c, r = new
            if c == "s":
                ref = slot_a(0, 0 if r != 2 else -s)
                return ref, ref
            here = own_blocks.at[not_same] if r != 2 else other.at[(-s) % NY - 1]
            return here, other.at[r - 1]
        if kind in ("Az", "Bz"):
            o, r = new[-1], new[1] if kind == "Az" else 0
            place = slot_a if kind == "Az" else slot_b
            if abs(o) == 1:
                there = place(0, r)
                if kind == "Bz":
                    return own_blocks.at[not_same + 1], there
                return (own_blocks.at[not_same] if r == 0 else other.at[r - 1]), there
            ref = place(0 if abs(o) == 2 else -s * (abs(o) - 2), r)
            return ref, ref
        ref = slot_b(new[2], 0 if kind == "By" else -s)
        return ref, ref

    def fold(found):
        found = found.reshape(-1, 2, 8, 256)
        return found[:, 0, :, :128] + found[:, 1, :, 128:]

    def product_a(o):
        at = pl.ds(at_z(o) * NY, NY)
        block = ga[at].reshape(NY * 16, W)
        pa[1, at] = fold(jnp.dot(block, pc[2], preferred_element_type=F32))
        send(("ra", o), pa.at[1, at], pa.at[2, at], dev(at_z(1), y))
        pa[0, at] = fold(jnp.dot(block, pc[0], preferred_element_type=F32))

    def product_b(r):
        at = pl.ds(at_y(r) * NZ, NZ)
        block = gb[at].reshape(NZ * 16, W)
        pb[1, at] = fold(jnp.dot(block, pc[3], preferred_element_type=F32))
        send(("rb", r), pb.at[1, at], pb.at[2, at], dev(at_z(-1), y))
        pb[0, at] = fold(jnp.dot(block, pc[1], preferred_element_type=F32))

    come = []

    def products(run, which):
        if not come:
            wait(("pu",), neighbours.at[0])
            turn(neighbours.at[0], 0, pc.at[2])
            wait(("pd",), neighbours.at[1])
            turn(neighbours.at[1], 0, pc.at[3])
        come.append(run)
        run(which)

    need_a = {o: 4 for o in range(NZ)}
    need_b = {r: 8 for r in range(NY)}
    for tag, sends in ORDER:
        if tag != ("own",):
            wait(tag, slot(tag))
        for link, new in sends:
            links = 1 if link[0] == "y" or abs(new[-1]) == 1 else 2
            step = links if link[1] == "+" else -links
            to = dev(at_z(step), y) if link[0] == "z" else dev(z, at_y(step))
            send(new, *ends_of(link, new), to)
        kind = tag[0]
        if kind in ("own", "Ay", "Az") and tag[1:2] != ("o",):
            o = tag[2] % NZ if kind == "Az" else 0
            need_a[o] -= 1
            if need_a[o] == 0:
                products(product_a, o)
        if kind in ("own", "Bz", "By", "Bo"):
            r = 2 if kind == "Bo" else 0 if kind != "By" else 3 if tag[1] == "+" else 1
            need_b[r] -= 1
            if need_b[r] == 0:
                products(product_b, r)
    assert not any(need_a.values()) and not any(need_b.values())

    for o in range(NZ):
        wait(("ra", o), pa.at[2, pl.ds(at_z(o - 1) * NY, NY)])
    for r in range(NY):
        wait(("rb", r), pb.at[2, pl.ds(at_y(r) * NZ, NZ)])
    for p in range(NT):
        pair = []
        for d in (2 * p, 2 * p + 1):
            i = (d % NY) * NZ + d // NY
            pair.append((pa[0, d] + pa[2, d]) + (pb[0, i] + pb[2, i]))
        sbuf[p] = jnp.concatenate(pair, axis=0)
    for r in range(1, NT):
        p = at_t(r)
        send(("p", r), sbuf.at[p], precv.at[me], (dp, p))
    precv[me] = sbuf[me]
    for r in range(1, NT):
        wait(("p", r), precv.at[at_t(-r)])
    projected = precv[0]
    for t in range(1, NT):
        projected = projected + precv[t]

    inner = lax.dot_general(
        projected, rows, nt, precision=lax.Precision.HIGHEST, preferred_element_type=F32
    )
    square = jnp.broadcast_to(jnp.sum(projected * projected, axis=1, keepdims=True), (16, 128))
    for i in range(NY):
        up_rows, lanes = slice((i // 2) * 8, (i // 2) * 8 + 8), slice((i % 2) * 128, (i % 2) * 128 + 128)
        y1s[i, 0] = inner[up_rows, lanes]
        y1s[i, 1] = square[up_rows, :]
    for r in range(1, NY):
        send(("y1", r), y1s.at[at_y(r)], y1r.at[y], dev(z, at_y(r)))
    y1r[y] = y1s[y]
    for r in range(1, NY):
        wait(("y1", r), y1r.at[at_y(-r)])
    z1r[z] = (y1r[0] + y1r[1]) + (y1r[2] + y1r[3])
    for r in range(1, NZ):
        send(("z1", r), z1r.at[z], z1r.at[z], dev(at_z(r), y))
    for r in range(1, NZ):
        wait(("tz", r), tqz.at[at_z(-r)])
    norm = tqz[0]
    for t in range(1, NZ):
        norm = norm + tqz[t]
    norm = jnp.where(lax.rem(y, 2) == 0, norm[0:1], norm[1:2])
    for r in range(1, NZ):
        wait(("z1", r), z1r.at[at_z(-r)])
    both = z1r[0]
    for t in range(1, NZ):
        both = both + z1r[t]
    fin[y] = math.sqrt(K) * both[0] * lax.rsqrt(both[1] + EPS) * lax.rsqrt(norm + EPS)
    for r in range(1, NY):
        send(("y2", r), fin.at[y], fin.at[y], dev(z, at_y(r)))
    for r in range(1, NY):
        wait(("y2", r), fin.at[at_y(-r)])
    for i in range(NY):
        out[(i // 2) * 8 : (i // 2) * 8 + 8, (i % 2) * 128 : (i % 2) * 128 + 128] = fin[i]
    for c in sent:
        c.wait_send()


def body(activations, cotangents, lengths, down, up, projection, target):
    vmem, hbm = pl.BlockSpec(memory_space=pltpu.VMEM), pl.BlockSpec(memory_space=pl.ANY)
    return pl.pallas_call(
        kernel,
        out_shape=jax.ShapeDtypeStruct((16, 256), F32),
        in_specs=[hbm] * 7,
        out_specs=vmem,
        scratch_shapes=[
            pltpu.VMEM((8, 128, 512), BF16),
            pltpu.VMEM((8, 128, 512), BF16),
            pltpu.SMEM((8,), jnp.int32),
            pltpu.VMEM((8, 512), BF16),
            pltpu.VMEM((8, 512), BF16),
            pltpu.VMEM((8192, 128), BF16),
            pltpu.VMEM((256, 128), BF16),
            pltpu.VMEM((4, W, 256), BF16),
            pltpu.VMEM((2, 2048, 128), BF16),
            pltpu.VMEM((4, 16, W), BF16),
            pltpu.VMEM((3, 16, W), BF16),
            pltpu.VMEM((32, 16, W), BF16),
            pltpu.VMEM((32, 16, W), BF16),
            pltpu.VMEM((16, 8, 128), F32),
            pltpu.VMEM((16, 8, 128), F32),
            pltpu.VMEM((16, 8, 128), F32),
            pltpu.VMEM((3, 32, 8, 128), F32),
            pltpu.VMEM((3, 32, 8, 128), F32),
            pltpu.VMEM((16, 16, 128), F32),
            pltpu.VMEM((16, 16, 128), F32),
            pltpu.VMEM((8, 128), F32),
            pltpu.VMEM((4, 8, 128), F32),
            pltpu.VMEM((8, 8, 128), F32),
            pltpu.VMEM((4, 2, 8, 128), F32),
            pltpu.VMEM((4, 2, 8, 128), F32),
            pltpu.VMEM((8, 2, 8, 128), F32),
            pltpu.VMEM((4, 8, 128), F32),
            pltpu.SemaphoreType.DMA((7,)),
            pltpu.SemaphoreType.DMA((len(TAGS),)),
            pltpu.SemaphoreType.DMA((len(TAGS),)),
        ],
        compiler_params=pltpu.CompilerParams(
            collective_id=0, has_side_effects=True, vmem_limit_bytes=60 * 1024 * 1024
        ),
    )(activations, cotangents, lengths, down.T, up, projection, target)


def solution(mesh):
    placed = (
        P("dp", None, "tensor"),
        P("dp", None, "tensor"),
        P("dp"),
        P("tensor", None),
        P(None, "tensor"),
        P("tensor", "dp"),
        P(None, "dp"),
    )
    return jax.shard_map(
        body, mesh=mesh, in_specs=placed, out_specs=P("tensor", None), check_vma=False
    )
```

```python
import heapq
import math

import jax
import jax.numpy as jnp
from jax import lax
from jax.experimental import pallas as pl
from jax.experimental.pallas import tpu as pltpu
from jax.sharding import PartitionSpec as P

MESH = pl.DeviceIdType.MESH
K = 4096
SCALE = 2.0
EPS = 1e-06
NZ, NY, NT = 8, 4, 16
W = 1024
F32, BF16 = jnp.float32, jnp.bfloat16


def onward(o, r):
    if o in (-1, 1):
        return [(3 * o, "z+" if o < 0 else "z-")]
    if o in (-2, 2) and (o < 0) == (r % 2 == 0):
        return [(4, "z+" if o < 0 else "z-")]
    return []


def follow(tag):
    kind = tag[0]
    if kind == "own":
        sends = [("y" + w, ("Ay", c, 3 if w == "+" else 1), 2) for c in "so" for w in "+-"]
        for o, links in ((1, 1), (2, 2)):
            sends += [("z+", ("Bz", -o), links), ("z-", ("Bz", o), links)]
        for o, links in ((1, 1), (2, 2)):
            sends += [("z+", ("Az", 0, -o), links), ("z-", ("Az", 0, o), links)]
        return sends + [("y+", ("By", "+", 0), 2), ("y-", ("By", "-", 0), 2)]
    if kind == "Ay":
        _, c, r = tag
        o = 2 if c == "s" else 1
        sends = [("z+", ("Az", r, -o), o), ("z-", ("Az", r, o), o)]
        if (c, r) in (("s", 3), ("o", 1)):
            sends = [("y+" if c == "s" else "y-", ("Ay", c, 2), 2)] + sends
        return sends
    if kind == "Az":
        return [(link, ("Az", tag[1], o), 2) for o, link in onward(tag[2], tag[1])]
    if kind == "Bz":
        on = [(link, ("Bz", o), 2) for o, link in onward(tag[1], 0)]
        return on + [("y+", ("By", "+", tag[1]), 2), ("y-", ("By", "-", tag[1]), 2)]
    if kind == "By" and (tag[2] % 2 == 0) == (tag[1] == "+"):
        return [("y" + tag[1], ("Bo", tag[1], tag[2]), 2)]
    return []


def plan():
    free = dict.fromkeys(("z+", "z-", "y+", "y-"), 0.0)
    heap, order, count = [(0.0, 0, ("own",))], [], 0
    while heap:
        now, _, tag = heapq.heappop(heap)
        sends = follow(tag)
        order.append((now, tag, [(link, new) for link, new, _ in sends]))
        for link, new, links in sends:
            count += 1
            free[link] = max(now, free[link]) + links * 0.655
            heapq.heappush(heap, (free[link] + 2.2 + 0.6 * links, count, new))
    return order


ORDER = [(tag, sends) for _, tag, sends in plan()]
CUTS = (10, 10, 8, 4)


def filled(tag):
    kind = tag[0]
    if kind == "own":
        return [(0, 0, 0), (1, 0, 0)]
    if kind == "Ay":
        return [(0, 0, tag[2])] if tag[1] == "s" else []
    if kind == "Az":
        return [(0, tag[2], tag[1])]
    if kind == "Bz":
        return [(1, tag[1], 0)]
    return [(1, tag[2], 2 if kind == "Bo" else 3 if tag[1] == "+" else 1)]


COME = [[b[1:] for tag, _ in ORDER for b in filled(tag) if b[0] == half] for half in (0, 1)]
STARTS = [sum(CUTS[:i]) for i in range(len(CUTS))]
TAGS = [tag for tag, _ in ORDER[1:]]
TAGS += [(k, r) for k in ("h", "f") for r in range(1, NT)]
TAGS += [(k, r) for k in ("y1", "ty") for r in range(1, NY)]
TAGS += [(k, r) for k in ("z1", "tz") for r in range(1, NZ)]
TAGS += [("pu",), ("pd",)] + [("p", i, r) for i in range(3) for r in range(NT) if i or r]
INDEX = {tag: i for i, tag in enumerate(TAGS)}


def kernel(
    act_in, cot_in, lengths_in, down_in, up_in, proj_in, target_in, out,
    act, cot, lengths, down, up, proj, target, pc, neighbours, own_blocks, other, ga, gb, hid, hrecv, facs, total, rounded, precv,
    tqz, along, zsum, lsem, ssem, rsem,
):
    dp, me = lax.axis_index("dp"), lax.axis_index("tensor")
    z, y = lax.div(dp, NY), lax.rem(dp, NY)
    parity = lax.rem(z, 2)

    def at_z(o):
        return lax.rem(z + (o % NZ), NZ)

    def at_y(o):
        return lax.rem(y + (o % NY), NY)

    def at_t(o):
        return lax.rem(me + (o % NT), NT)

    def dev(zz, yy):
        return (zz * NY + yy, me)

    def copy(tag, src, dst, device):
        i = INDEX[tag]
        return pltpu.make_async_remote_copy(
            src_ref=src, dst_ref=dst, send_sem=ssem.at[i], recv_sem=rsem.at[i],
            device_id=device, device_id_type=MESH,
        )

    sent = []

    def send(tag, src, dst, device):
        c = copy(tag, src, dst, device)
        c.start()
        sent.append(c)

    def wait(tag, ref):
        copy(tag, ref, ref, dev(at_z(1), y)).wait_recv()

    here_y = pl.ds(pl.multiple_of(y * 128, 128), 128)
    ends = (
        (down_in, down), (act_in, act), (up_in, up), (cot_in, cot),
        (target_in, target.at[:, here_y]), (lengths_in, lengths), (proj_in, proj),
    )
    loads = [pltpu.make_async_copy(a, b, lsem.at[i]) for i, (a, b) in enumerate(ends)]
    for c in loads:
        c.start()

    barrier = pltpu.get_barrier_semaphore()
    partners = [(dp, at_t(r)) for r in range(1, NT)]
    partners += [dev(at_z(o), y) for o in range(1, NZ)] + [dev(z, at_y(o)) for o in range(1, NY)]
    partners += [(at_z(o) * NY + y, at_t(r)) for o in (-1, 1) for r in range(1, NT)]
    for p in partners:
        pl.semaphore_signal(barrier, inc=1, device_id=p, device_id_type=MESH)

    nt = (((1,), (1,)), ((), ()))
    loads[0].wait()
    loads[1].wait()
    for e in range(8):
        hid[8 + e] = lax.dot_general(down[...], act[e], nt, preferred_element_type=F32)
    loads[2].wait()
    loads[3].wait()
    for e in range(8):
        hid[e] = lax.dot_general(up[...], cot[e], nt, preferred_element_type=F32)
    pl.semaphore_wait(barrier, len(partners))
    loads[6].wait()
    theirs = pl.multiple_of((1 - parity) * 4096, 4096)
    for r in range(1, NT):
        p = at_t(r)
        send(("h", r), hid.at[p], hrecv.at[me], (dp, p))
    send(("pu",), proj.at[pl.ds(theirs, 2048)], neighbours.at[0], dev(at_z(-1), y))
    send(("pd",), proj.at[pl.ds(theirs + 2048, 2048)], neighbours.at[1], dev(at_z(1), y))
    hrecv[me] = hid[me]

    loads[4].wait()
    for r in range(1, NY):
        send(("ty", r), target.at[:, here_y], target.at[:, here_y], dev(z, at_y(r)))

    q = lax.broadcasted_iota(jnp.int32, (256, 256), 0)
    c = lax.broadcasted_iota(jnp.int32, (256, 256), 1)
    swap = jnp.where(c == lax.rem(q, 16) * 16 + lax.div(q, 16), 1.0, 0.0).astype(BF16)

    def turn(source, first, to):
        def step(b, carry):
            block = source[pl.ds(pl.multiple_of(first + b * 256, 256), 256), :]
            moved = jnp.dot(swap, block, preferred_element_type=F32).astype(BF16)
            for j in range(16):
                at = pl.ds(pl.multiple_of(b * 16 + (j % 8) * 128, 16), 16)
                to[at, (j // 8) * 128 : (j // 8) * 128 + 128] = moved[j * 16 : j * 16 + 16]
            return carry

        lax.fori_loop(0, 8, step, 0, unroll=True)

    mine = pl.multiple_of(parity * 4096, 4096)
    turn(proj, mine, pc.at[0])

    for r in range(1, NT):
        wait(("h", r), hrecv.at[at_t(-r)])
    hidden = hrecv[0]
    for t in range(1, NT):
        hidden = hidden + hrecv[t]
    loads[5].wait()
    token = lax.broadcasted_iota(jnp.int32, (8, 128), 1)
    facs[me] = jnp.where(token < lengths[lax.rem(me, 8)], SCALE, 0.0) * hidden
    for r in range(1, NT):
        send(("f", r), facs.at[me], facs.at[me], (dp, at_t(r)))

    turn(proj, mine + 2048, pc.at[1])
    total[...] = jnp.zeros((3, 32, 8, 128), F32)

    for r in range(1, NT):
        wait(("f", r), facs.at[at_t(-r)])
    own = lax.broadcasted_iota(jnp.int32, (8, 8, 128), 1)
    grads = []
    for a, data in ((0, act), (1, cot)):
        parts = []
        for e in range(8):
            spread = jnp.broadcast_to(facs[a * 8 + e][:, None, :], (8, 8, 128))
            parts.append(jnp.where(own == e, spread, 0.0).reshape(64, 128).astype(BF16))
        left = jnp.concatenate(parts, axis=1)
        grads.append(jnp.dot(left, data[...].reshape(1024, 512), preferred_element_type=F32))
    for j in range(8):
        tile = jnp.concatenate([g[j * 8 : j * 8 + 8] for g in grads], axis=0).astype(BF16)
        for i in range(4):
            own_blocks[i, :, j * 128 : j * 128 + 128] = tile[:, i * 128 : i * 128 + 128]
    same, not_same = 2 * parity, 2 - 2 * parity
    ga[dp] = own_blocks[same]
    gb[y * NZ + z] = own_blocks[same + 1]

    def slot_index_a(o, r):
        return at_z(o) * NY + at_y(r)

    def slot_index_b(o, r):
        return at_y(r) * NZ + at_z(o)

    def slot_a(o, r):
        return ga.at[slot_index_a(o, r)]

    def slot_b(o, r):
        return gb.at[slot_index_b(o, r)]

    def slot(tag):
        kind = tag[0]
        if kind == "Ay":
            return slot_a(0, tag[2]) if tag[1] == "s" else other.at[tag[2] - 1]
        if kind == "Az":
            return slot_a(tag[2], tag[1])
        if kind == "Bz":
            return slot_b(tag[1], 0)
        return slot_b(tag[2], 2 if kind == "Bo" else 3 if tag[1] == "+" else 1)

    def ends_of(link, new):
        kind = new[0]
        s = 1 if link[1] == "+" else -1
        if kind == "Ay":
            _, c, r = new
            if c == "s":
                ref = slot_a(0, 0 if r != 2 else -s)
                return ref, ref
            here = own_blocks.at[not_same] if r != 2 else other.at[(-s) % NY - 1]
            return here, other.at[r - 1]
        if kind in ("Az", "Bz"):
            o, r = new[-1], new[1] if kind == "Az" else 0
            place = slot_a if kind == "Az" else slot_b
            if abs(o) == 1:
                there = place(0, r)
                if kind == "Bz":
                    return own_blocks.at[not_same + 1], there
                return (own_blocks.at[not_same] if r == 0 else other.at[r - 1]), there
            ref = place(0 if abs(o) == 2 else -s * (abs(o) - 2), r)
            return ref, ref
        ref = slot_b(new[2], 0 if kind == "By" else -s)
        return ref, ref

    def fold(found):
        found = found.reshape(-1, 2, 8, 256)
        return found[:, 0, :, :128] + found[:, 1, :, 128:]

    def product(half, first, count):
        gathered, slots = ((ga, slot_index_a), (gb, slot_index_b))[half]
        places = COME[half][first : first + count]
        block = jnp.concatenate([gathered[slots(o, r)] for o, r in places], axis=0)
        mine = fold(jnp.dot(block, pc[half], preferred_element_type=F32))
        next_one = fold(jnp.dot(block, pc[2 + half], preferred_element_type=F32))
        for i, (o, r) in enumerate(places):
            at = slot_index_a(o, r)
            total[0, at] += mine[i]
            total[1 + half, at] = next_one[i]

    def validation():
        for r in range(1, NY):
            lanes = pl.ds(pl.multiple_of(at_y(-r) * 128, 128), 128)
            wait(("ty", r), target.at[:, lanes])
        ones = jnp.ones((8, 512), F32)
        wide = target[...].astype(F32)
        tqz[z] = lax.dot_general(
            ones, wide * wide, nt, precision=lax.Precision.HIGHEST, preferred_element_type=F32
        )
        for r in range(1, NZ):
            send(("tz", r), tqz.at[z], tqz.at[z], dev(at_z(r), y))

    seen = [0, 0]
    for turn_of, (tag, sends) in enumerate(ORDER):
        if tag != ("own",):
            wait(tag, slot(tag))
        for link, new in sends:
            links = 1 if link[0] == "y" or abs(new[-1]) == 1 else 2
            step = links if link[1] == "+" else -links
            to = dev(at_z(step), y) if link[0] == "z" else dev(z, at_y(step))
            send(new, *ends_of(link, new), to)
        if turn_of == 8:
            validation()
        for half, _, _ in filled(tag):
            seen[half] += 1
            for first, count in zip(STARTS, CUTS):
                if seen[half] == first + count:
                    if first == 0:
                        wait(("pd",) if half else ("pu",), neighbours.at[half])
                        turn(neighbours.at[half], 0, pc.at[2 + half])
                    product(half, first, count)

    for i, o in ((1, 1), (2, -1), (0, 0)):
        rounded[i] = total[i].reshape(16, 16, 128).astype(BF16)
        for r in range(NT):
            if i or r:
                p = at_t(r)
                send(("p", i, r), rounded.at[i, p], precv.at[i, me], (at_z(o) * NY + y, p))
    precv[0, me] = rounded[0, me]
    projected = jnp.zeros((16, 128), F32)
    for i in (1, 2, 0):
        for r in range(NT):
            if i or r:
                wait(("p", i, r), precv.at[i, at_t(-r)])
    for i in range(3):
        for t in range(NT):
            projected = projected + precv[i, t].astype(F32)
    along[y] = projected
    for r in range(1, NY):
        send(("y1", r), along.at[y], along.at[y], dev(z, at_y(r)))
    for r in range(1, NY):
        wait(("y1", r), along.at[at_y(-r)])
    wide = jnp.concatenate([along[i] for i in range(NY)], axis=1)
    high = wide.astype(BF16)
    rest = wide - high.astype(F32)
    middle = rest.astype(BF16)
    low = (rest - middle.astype(F32)).astype(BF16)
    three = lax.dot_general(
        jnp.concatenate([high, middle, low], axis=0), target[...], nt, preferred_element_type=F32
    )
    zsum[z, :, :256] = ((three[32:] + three[16:32]) + three[:16]).astype(BF16)
    square = jnp.sum(wide * wide, axis=1, keepdims=True)
    zsum[z, :, 256:] = jnp.broadcast_to(square, (16, 128)).astype(BF16)
    for r in range(1, NZ):
        send(("z1", r), zsum.at[z], zsum.at[z], dev(at_z(r), y))
    for r in range(1, NZ):
        wait(("tz", r), tqz.at[at_z(-r)])
    norm = tqz[0]
    for t in range(1, NZ):
        norm = norm + tqz[t]
    norm = math.sqrt(K) * lax.rsqrt(norm[0:1] + EPS)
    for r in range(1, NZ):
        wait(("z1", r), zsum.at[at_z(-r)])
    both = zsum[0].astype(F32)
    for t in range(1, NZ):
        both = both + zsum[t].astype(F32)
    own_norm = lax.rsqrt(both[:, 256:] + EPS)
    out[:, :128] = both[:, :128] * own_norm * norm[:, :128]
    out[:, 128:] = both[:, 128:256] * own_norm * norm[:, 128:]
    for c in sent:
        c.wait_send()


def body(activations, cotangents, lengths, down, up, projection, target):
    vmem, hbm = pl.BlockSpec(memory_space=pltpu.VMEM), pl.BlockSpec(memory_space=pl.ANY)
    return pl.pallas_call(
        kernel,
        out_shape=jax.ShapeDtypeStruct((16, 256), F32),
        in_specs=[hbm] * 7,
        out_specs=vmem,
        scratch_shapes=[
            pltpu.VMEM((8, 128, 512), BF16),
            pltpu.VMEM((8, 128, 512), BF16),
            pltpu.SMEM((8,), jnp.int32),
            pltpu.VMEM((8, 512), BF16),
            pltpu.VMEM((8, 512), BF16),
            pltpu.VMEM((8192, 128), BF16),
            pltpu.VMEM((256, 512), BF16),
            pltpu.VMEM((4, W, 256), BF16),
            pltpu.VMEM((2, 2048, 128), BF16),
            pltpu.VMEM((4, 16, W), BF16),
            pltpu.VMEM((3, 16, W), BF16),
            pltpu.VMEM((32, 16, W), BF16),
            pltpu.VMEM((32, 16, W), BF16),
            pltpu.VMEM((16, 8, 128), F32),
            pltpu.VMEM((16, 8, 128), F32),
            pltpu.VMEM((16, 8, 128), F32),
            pltpu.VMEM((3, 32, 8, 128), F32),
            pltpu.VMEM((3, 16, 16, 128), BF16),
            pltpu.VMEM((3, 16, 16, 128), BF16),
            pltpu.VMEM((8, 8, 256), F32),
            pltpu.VMEM((4, 16, 128), F32),
            pltpu.VMEM((8, 16, 384), BF16),
            pltpu.SemaphoreType.DMA((7,)),
            pltpu.SemaphoreType.DMA((len(TAGS),)),
            pltpu.SemaphoreType.DMA((len(TAGS),)),
        ],
        compiler_params=pltpu.CompilerParams(
            collective_id=0, has_side_effects=True, vmem_limit_bytes=60 * 1024 * 1024
        ),
    )(activations, cotangents, lengths, down.T, up, projection, target)


def solution(mesh):
    placed = (
        P("dp", None, "tensor"),
        P("dp", None, "tensor"),
        P("dp"),
        P("tensor", None),
        P(None, "tensor"),
        P("tensor", "dp"),
        P(None, "dp"),
    )
    return jax.shard_map(
        body, mesh=mesh, in_specs=placed, out_specs=P("tensor", None), check_vma=False
    )
```

```python
import heapq
import math

import jax
import jax.numpy as jnp
from jax import lax
from jax.experimental import pallas as pl
from jax.experimental.pallas import tpu as pltpu
from jax.sharding import PartitionSpec as P

MESH = pl.DeviceIdType.MESH
K = 4096
SCALE = 2.0
EPS = 1e-06
NZ, NY, NT = 8, 4, 16
W = 1024
F32, BF16 = jnp.float32, jnp.bfloat16


def onward(o, r):
    if o in (-1, 1):
        return [(3 * o, "z+" if o < 0 else "z-")]
    if o in (-2, 2) and (o < 0) == (r % 2 == 0):
        return [(4, "z+" if o < 0 else "z-")]
    return []


def follow(tag):
    kind = tag[0]
    if kind == "own":
        sends = [("y" + w, ("Ay", c, 3 if w == "+" else 1), 2) for c in "so" for w in "+-"]
        for o, links in ((1, 1), (2, 2)):
            sends += [("z+", ("Bz", -o), links), ("z-", ("Bz", o), links)]
        for o, links in ((1, 1), (2, 2)):
            sends += [("z+", ("Az", 0, -o), links), ("z-", ("Az", 0, o), links)]
        return sends + [("y+", ("By", "+", 0), 2), ("y-", ("By", "-", 0), 2)]
    if kind == "Ay":
        _, c, r = tag
        o = 2 if c == "s" else 1
        sends = [("z+", ("Az", r, -o), o), ("z-", ("Az", r, o), o)]
        if (c, r) in (("s", 3), ("o", 1)):
            sends = [("y+" if c == "s" else "y-", ("Ay", c, 2), 2)] + sends
        return sends
    if kind == "Az":
        return [(link, ("Az", tag[1], o), 2) for o, link in onward(tag[2], tag[1])]
    if kind == "Bz":
        on = [(link, ("Bz", o), 2) for o, link in onward(tag[1], 0)]
        return on + [("y+", ("By", "+", tag[1]), 2), ("y-", ("By", "-", tag[1]), 2)]
    if kind == "By" and (tag[2] % 2 == 0) == (tag[1] == "+"):
        return [("y" + tag[1], ("Bo", tag[1], tag[2]), 2)]
    return []


def left(tag):
    return max((n * 1.255 + 2.2 + left(new) for _, new, n in follow(tag)), default=0.0)


BUSY, AHEAD = 2.0, 2.5


def plan():
    free = {"z+": BUSY, "z-": BUSY, "y+": 0.0, "y-": 0.0}
    waiting = {link: [] for link in free}
    heap, count, came, starts = [(0.0, 0, ("own",)), (BUSY, 1, None)], 1, {}, []
    while heap:
        now = heap[0][0]
        while heap and heap[0][0] <= now + 1e-6:
            tag = heapq.heappop(heap)[2]
            if tag is not None:
                came[tag] = now
                for link, new, links in follow(tag):
                    count += 1
                    heapq.heappush(waiting[link], (-left(new), count, new, links, now))
        for link, line in waiting.items():
            if line and free[link] <= now + 1e-6:
                _, _, new, links, since = heapq.heappop(line)
                free[link] = now + links * 0.655
                starts.append((max(since, now - AHEAD), now, link, new))
                count += 2
                heapq.heappush(heap, (free[link], count - 1, None))
                heapq.heappush(heap, (free[link] + 2.2 + 0.6 * links, count, new))
    order = [(tag, []) for tag in came]
    times = list(came.values())
    for issue, _, link, new in sorted(starts, key=lambda x: x[1]):
        order[sum(t <= issue + 1e-6 for t in times) - 1][1].append((link, new))
    return order


ORDER = plan()
CUTS = (10, 10, 8, 4)


def filled(tag):
    kind = tag[0]
    if kind == "own":
        return [(0, 0, 0), (1, 0, 0)]
    if kind == "Ay":
        return [(0, 0, tag[2])] if tag[1] == "s" else []
    if kind == "Az":
        return [(0, tag[2], tag[1])]
    if kind == "Bz":
        return [(1, tag[1], 0)]
    return [(1, tag[2], 2 if kind == "Bo" else 3 if tag[1] == "+" else 1)]


COME = [[b[1:] for tag, _ in ORDER for b in filled(tag) if b[0] == half] for half in (0, 1)]
STARTS = [sum(CUTS[:i]) for i in range(len(CUTS))]
TAGS = [tag for tag, _ in ORDER[1:]]
TAGS += [(k, r) for k in ("h", "f") for r in range(1, NT)]
TAGS += [(k, r) for k in ("y1", "ty") for r in range(1, NY)]
TAGS += [(k, r) for k in ("z1", "tz") for r in range(1, NZ)]
TAGS += [("pu",), ("pd",)] + [("c",)] + [("p", i, r) for i in range(3) for r in range(8) if i or r]
INDEX = {tag: i for i, tag in enumerate(TAGS)}


def kernel(
    act_in, cot_in, lengths_in, down_in, up_in, proj_in, target_in, out,
    act, cot, lengths, down, up, proj, target, pc, neighbours, own_blocks, other, ga, gb, hid, hrecv, facs, total, twin, rounded, precv,
    tqz, along, zsum, lsem, ssem, rsem,
):
    dp, me = lax.axis_index("dp"), lax.axis_index("tensor")
    z, y = lax.div(dp, NY), lax.rem(dp, NY)
    parity = lax.rem(z, 2)

    def at_z(o):
        return lax.rem(z + (o % NZ), NZ)

    def at_y(o):
        return lax.rem(y + (o % NY), NY)

    def at_t(o):
        return lax.rem(me + (o % NT), NT)

    def dev(zz, yy):
        return (zz * NY + yy, me)

    def copy(tag, src, dst, device):
        i = INDEX[tag]
        return pltpu.make_async_remote_copy(
            src_ref=src, dst_ref=dst, send_sem=ssem.at[i], recv_sem=rsem.at[i],
            device_id=device, device_id_type=MESH,
        )

    sent = []

    def send(tag, src, dst, device):
        c = copy(tag, src, dst, device)
        c.start()
        sent.append(c)

    def settle(some):
        for c in sent[:some]:
            c.wait_send()
        del sent[:some]

    def wait(tag, ref):
        copy(tag, ref, ref, dev(at_z(1), y)).wait_recv()

    here_y = pl.ds(pl.multiple_of(y * 128, 128), 128)
    ends = (
        (down_in, down), (act_in, act), (up_in, up), (cot_in, cot),
        (target_in, target.at[:, here_y]), (lengths_in, lengths), (proj_in, proj),
    )
    loads = [pltpu.make_async_copy(a, b, lsem.at[i]) for i, (a, b) in enumerate(ends)]
    for c in loads:
        c.start()

    barrier = pltpu.get_barrier_semaphore()
    partners = [(dp, at_t(r)) for r in range(1, NT)]
    partners += [dev(at_z(o), y) for o in range(1, NZ)] + [dev(z, at_y(o)) for o in range(1, NY)]
    partners += [(at_z(o) * NY + y, at_t(r)) for o in (-1, 1) for r in range(2, NT, 2)]
    for p in partners:
        pl.semaphore_signal(barrier, inc=1, device_id=p, device_id_type=MESH)

    nt = (((1,), (1,)), ((), ()))
    loads[0].wait()
    loads[1].wait()
    for e in range(8):
        hid[8 + e] = lax.dot_general(down[...], act[e], nt, preferred_element_type=F32)
    loads[2].wait()
    loads[3].wait()
    for e in range(8):
        hid[e] = lax.dot_general(up[...], cot[e], nt, preferred_element_type=F32)
    pl.semaphore_wait(barrier, len(partners))
    loads[6].wait()
    theirs = pl.multiple_of((1 - parity) * 4096, 4096)
    for r in range(1, NT):
        p = at_t(r)
        send(("h", r), hid.at[p], hrecv.at[me], (dp, p))
    send(("pu",), proj.at[pl.ds(theirs, 2048)], neighbours.at[0], dev(at_z(-1), y))
    send(("pd",), proj.at[pl.ds(theirs + 2048, 2048)], neighbours.at[1], dev(at_z(1), y))
    hrecv[me] = hid[me]

    loads[4].wait()
    for r in range(1, NY):
        send(("ty", r), target.at[:, here_y], target.at[:, here_y], dev(z, at_y(r)))

    q = lax.broadcasted_iota(jnp.int32, (256, 256), 0)
    c = lax.broadcasted_iota(jnp.int32, (256, 256), 1)
    swap = jnp.where(c == lax.rem(q, 16) * 16 + lax.div(q, 16), 1.0, 0.0).astype(BF16)

    def turn(source, first, to):
        def step(b, carry):
            block = source[pl.ds(pl.multiple_of(first + b * 256, 256), 256), :]
            moved = jnp.dot(swap, block, preferred_element_type=F32).astype(BF16)
            for j in range(16):
                at = pl.ds(pl.multiple_of(b * 16 + (j % 8) * 128, 16), 16)
                to[at, (j // 8) * 128 : (j // 8) * 128 + 128] = moved[j * 16 : j * 16 + 16]
            return carry

        lax.fori_loop(0, 8, step, 0, unroll=True)

    mine = pl.multiple_of(parity * 4096, 4096)
    turn(proj, mine, pc.at[0])

    for r in range(1, NT):
        wait(("h", r), hrecv.at[at_t(-r)])
    hidden = hrecv[0]
    for t in range(1, NT):
        hidden = hidden + hrecv[t]
    loads[5].wait()
    token = lax.broadcasted_iota(jnp.int32, (8, 128), 1)
    facs[me] = jnp.where(token < lengths[lax.rem(me, 8)], SCALE, 0.0) * hidden
    for r in range(1, NT):
        send(("f", r), facs.at[me], facs.at[me], (dp, at_t(r)))

    settle(NT - 1)
    turn(proj, mine + 2048, pc.at[1])
    total[...] = jnp.zeros((2, 3, 8, 2, 8, 128), F32)

    for r in range(1, NT):
        wait(("f", r), facs.at[at_t(-r)])
    own = lax.broadcasted_iota(jnp.int32, (8, 8, 128), 1)
    grads = []
    for a, data in ((0, act), (1, cot)):
        parts = []
        for e in range(8):
            spread = jnp.broadcast_to(facs[a * 8 + e][:, None, :], (8, 8, 128))
            parts.append(jnp.where(own == e, spread, 0.0).reshape(64, 128).astype(BF16))
        left = jnp.concatenate(parts, axis=1)
        grads.append(jnp.dot(left, data[...].reshape(1024, 512), preferred_element_type=F32))
    for j in range(8):
        tile = jnp.concatenate([g[j * 8 : j * 8 + 8] for g in grads], axis=0).astype(BF16)
        for i in range(4):
            own_blocks[i, :, j * 128 : j * 128 + 128] = tile[:, i * 128 : i * 128 + 128]
    same, not_same = 2 * parity, 2 - 2 * parity
    ga[dp] = own_blocks[same]
    gb[y * NZ + z] = own_blocks[same + 1]

    def slot_index_a(o, r):
        return at_z(o) * NY + at_y(r)

    def slot_index_b(o, r):
        return at_y(r) * NZ + at_z(o)

    def slot_a(o, r):
        return ga.at[slot_index_a(o, r)]

    def slot_b(o, r):
        return gb.at[slot_index_b(o, r)]

    def slot(tag):
        kind = tag[0]
        if kind == "Ay":
            return slot_a(0, tag[2]) if tag[1] == "s" else other.at[tag[2] - 1]
        if kind == "Az":
            return slot_a(tag[2], tag[1])
        if kind == "Bz":
            return slot_b(tag[1], 0)
        return slot_b(tag[2], 2 if kind == "Bo" else 3 if tag[1] == "+" else 1)

    def ends_of(link, new):
        kind = new[0]
        s = 1 if link[1] == "+" else -1
        if kind == "Ay":
            _, c, r = new
            if c == "s":
                ref = slot_a(0, 0 if r != 2 else -s)
                return ref, ref
            here = own_blocks.at[not_same] if r != 2 else other.at[(-s) % NY - 1]
            return here, other.at[r - 1]
        if kind in ("Az", "Bz"):
            o, r = new[-1], new[1] if kind == "Az" else 0
            place = slot_a if kind == "Az" else slot_b
            if abs(o) == 1:
                there = place(0, r)
                if kind == "Bz":
                    return own_blocks.at[not_same + 1], there
                return (own_blocks.at[not_same] if r == 0 else other.at[r - 1]), there
            ref = place(0 if abs(o) == 2 else -s * (abs(o) - 2), r)
            return ref, ref
        ref = slot_b(new[2], 0 if kind == "By" else -s)
        return ref, ref

    def fold(found):
        found = found.reshape(-1, 2, 8, 256)
        return found[:, 0, :, :128] + found[:, 1, :, 128:]

    def product(half, first, count):
        gathered, slots = ((ga, slot_index_a), (gb, slot_index_b))[half]
        places = COME[half][first : first + count]
        block = jnp.concatenate([gathered[slots(o, r)] for o, r in places], axis=0)
        mine = fold(jnp.dot(block, pc[half], preferred_element_type=F32))
        next_one = fold(jnp.dot(block, pc[2 + half], preferred_element_type=F32))
        for i, (o, r) in enumerate(places):
            core_of, pair = lax.div(at_y(r), 2), lax.rem(at_y(r), 2)
            total[core_of, 0, at_z(o), pair] += mine[i]
            total[core_of, 1 + half, at_z(o), pair] = next_one[i]

    def validation():
        for r in range(1, NY):
            lanes = pl.ds(pl.multiple_of(at_y(-r) * 128, 128), 128)
            wait(("ty", r), target.at[:, lanes])
        ones = jnp.ones((8, 512), F32)
        wide = target[...].astype(F32)
        tqz[z] = lax.dot_general(
            ones, wide * wide, nt, precision=lax.Precision.HIGHEST, preferred_element_type=F32
        )
        for r in range(1, NZ):
            send(("tz", r), tqz.at[z], tqz.at[z], dev(at_z(r), y))

    seen = [0, 0]
    for turn_of, (tag, sends) in enumerate(ORDER):
        if tag != ("own",):
            wait(tag, slot(tag))
        for link, new in sends:
            links = 1 if link[0] == "y" or abs(new[-1]) == 1 else 2
            step = links if link[1] == "+" else -links
            to = dev(at_z(step), y) if link[0] == "z" else dev(z, at_y(step))
            send(new, *ends_of(link, new), to)
        if turn_of == 8:
            validation()
        for half, _, _ in filled(tag):
            seen[half] += 1
            for first, count in zip(STARTS, CUTS):
                if seen[half] == first + count:
                    if first == 0:
                        wait(("pd",) if half else ("pu",), neighbours.at[half])
                        turn(neighbours.at[half], 0, pc.at[2 + half])
                    product(half, first, count)

    core, spot = lax.rem(me, 2), lax.div(me, 2)
    send(("c",), total.at[1 - core], twin, (dp, me + 1 - 2 * core))
    wait(("c",), twin)
    for i, o in ((1, 1), (2, -1), (0, 0)):
        both_cores = total[core, i] + twin[i]
        rounded[i] = both_cores.reshape(8, 16, 128).astype(BF16)
        for r in range(8):
            if i or r:
                q = lax.rem(spot + r, 8)
                to = (at_z(o) * NY + y, q * 2 + core)
                send(("p", i, r), rounded.at[i, q], precv.at[i, spot], to)
    settle(len(sent))
    precv[0, spot] = rounded[0, spot]
    projected = jnp.zeros((16, 128), F32)
    for i in (1, 2, 0):
        for r in range(8):
            if i or r:
                wait(("p", i, r), precv.at[i, lax.rem(spot + 8 - r, 8)])
    for i in range(3):
        for t in range(8):
            projected = projected + precv[i, t].astype(F32)
    along[y] = projected
    for r in range(1, NY):
        send(("y1", r), along.at[y], along.at[y], dev(z, at_y(r)))
    for r in range(1, NY):
        wait(("y1", r), along.at[at_y(-r)])
    wide = jnp.concatenate([along[i] for i in range(NY)], axis=1)
    high = wide.astype(BF16)
    rest = wide - high.astype(F32)
    middle = rest.astype(BF16)
    low = (rest - middle.astype(F32)).astype(BF16)
    three = lax.dot_general(
        jnp.concatenate([high, middle, low], axis=0), target[...], nt, preferred_element_type=F32
    )
    zsum[z, :, :256] = ((three[32:] + three[16:32]) + three[:16]).astype(BF16)
    square = jnp.sum(wide * wide, axis=1, keepdims=True)
    zsum[z, :, 256:] = jnp.broadcast_to(square, (16, 128)).astype(BF16)
    for r in range(1, NZ):
        send(("z1", r), zsum.at[z], zsum.at[z], dev(at_z(r), y))
    settle(len(sent) - NZ + 1)
    for r in range(1, NZ):
        wait(("tz", r), tqz.at[at_z(-r)])
    norm = tqz[0]
    for t in range(1, NZ):
        norm = norm + tqz[t]
    norm = math.sqrt(K) * lax.rsqrt(norm[0:1] + EPS)
    for r in range(1, NZ):
        wait(("z1", r), zsum.at[at_z(-r)])
    both = zsum[0].astype(F32)
    for t in range(1, NZ):
        both = both + zsum[t].astype(F32)
    own_norm = lax.rsqrt(both[:, 256:] + EPS)
    out[:, :128] = both[:, :128] * own_norm * norm[:, :128]
    out[:, 128:] = both[:, 128:256] * own_norm * norm[:, 128:]
    settle(len(sent))


def body(activations, cotangents, lengths, down, up, projection, target):
    vmem, hbm = pl.BlockSpec(memory_space=pltpu.VMEM), pl.BlockSpec(memory_space=pl.ANY)
    return pl.pallas_call(
        kernel,
        out_shape=jax.ShapeDtypeStruct((16, 256), F32),
        in_specs=[hbm] * 7,
        out_specs=vmem,
        scratch_shapes=[
            pltpu.VMEM((8, 128, 512), BF16),
            pltpu.VMEM((8, 128, 512), BF16),
            pltpu.SMEM((8,), jnp.int32),
            pltpu.VMEM((8, 512), BF16),
            pltpu.VMEM((8, 512), BF16),
            pltpu.VMEM((8192, 128), BF16),
            pltpu.VMEM((256, 512), BF16),
            pltpu.VMEM((4, W, 256), BF16),
            pltpu.VMEM((2, 2048, 128), BF16),
            pltpu.VMEM((4, 16, W), BF16),
            pltpu.VMEM((3, 16, W), BF16),
            pltpu.VMEM((32, 16, W), BF16),
            pltpu.VMEM((32, 16, W), BF16),
            pltpu.VMEM((16, 8, 128), F32),
            pltpu.VMEM((16, 8, 128), F32),
            pltpu.VMEM((16, 8, 128), F32),
            pltpu.VMEM((2, 3, 8, 2, 8, 128), F32),
            pltpu.VMEM((3, 8, 2, 8, 128), F32),
            pltpu.VMEM((3, 8, 16, 128), BF16),
            pltpu.VMEM((3, 8, 16, 128), BF16),
            pltpu.VMEM((8, 8, 256), F32),
            pltpu.VMEM((4, 16, 128), F32),
            pltpu.VMEM((8, 16, 384), BF16),
            pltpu.SemaphoreType.DMA((7,)),
            pltpu.SemaphoreType.DMA((len(TAGS),)),
            pltpu.SemaphoreType.DMA((len(TAGS),)),
        ],
        compiler_params=pltpu.CompilerParams(
            collective_id=0, has_side_effects=True, vmem_limit_bytes=60 * 1024 * 1024
        ),
    )(activations, cotangents, lengths, down.T, up, projection, target)


def solution(mesh):
    placed = (
        P("dp", None, "tensor"),
        P("dp", None, "tensor"),
        P("dp"),
        P("tensor", None),
        P(None, "tensor"),
        P("tensor", "dp"),
        P(None, "dp"),
    )
    return jax.shard_map(
        body, mesh=mesh, in_specs=placed, out_specs=P("tensor", None), check_vma=False
    )
```

```python
import heapq
import math

import jax
import jax.numpy as jnp
from jax import lax
from jax.experimental import pallas as pl
from jax.experimental.pallas import tpu as pltpu
from jax.sharding import PartitionSpec as P

MESH = pl.DeviceIdType.MESH
K = 4096
SCALE = 2.0
EPS = 1e-06
NZ, NY, NT = 8, 4, 16
W = 1024
F32, BF16 = jnp.float32, jnp.bfloat16


def onward(o, r):
    if o in (-1, 1):
        return [(3 * o, "z+" if o < 0 else "z-")]
    if o in (-2, 2) and (o < 0) == (r % 2 == 0):
        return [(4, "z+" if o < 0 else "z-")]
    return []


def follow(tag):
    kind = tag[0]
    if kind == "own":
        sends = [("y" + w, ("Ay", c, 3 if w == "+" else 1), 2) for c in "so" for w in "+-"]
        for o, links in ((1, 1), (2, 2)):
            sends += [("z+", ("Bz", -o), links), ("z-", ("Bz", o), links)]
        for o, links in ((1, 1), (2, 2)):
            sends += [("z+", ("Az", 0, -o), links), ("z-", ("Az", 0, o), links)]
        return sends + [("y+", ("By", "+", 0), 2), ("y-", ("By", "-", 0), 2)]
    if kind == "Ay":
        _, c, r = tag
        o = 2 if c == "s" else 1
        sends = [("z+", ("Az", r, -o), o), ("z-", ("Az", r, o), o)]
        if (c, r) in (("s", 3), ("o", 1)):
            sends = [("y+" if c == "s" else "y-", ("Ay", c, 2), 2)] + sends
        return sends
    if kind == "Az":
        return [(link, ("Az", tag[1], o), 2) for o, link in onward(tag[2], tag[1])]
    if kind == "Bz":
        on = [(link, ("Bz", o), 2) for o, link in onward(tag[1], 0)]
        return on + [("y+", ("By", "+", tag[1]), 2), ("y-", ("By", "-", tag[1]), 2)]
    if kind == "By" and (tag[2] % 2 == 0) == (tag[1] == "+"):
        return [("y" + tag[1], ("Bo", tag[1], tag[2]), 2)]
    return []


def left(tag):
    return max((n * 1.255 + 2.2 + left(new) for _, new, n in follow(tag)), default=0.0)


BUSY, AHEAD = 2.0, 2.5


def plan():
    free = {"z+": BUSY, "z-": BUSY, "y+": 0.0, "y-": 0.0}
    waiting = {link: [] for link in free}
    heap, count, came, starts = [(0.0, 0, ("own",)), (BUSY, 1, None)], 1, {}, []
    while heap:
        now = heap[0][0]
        while heap and heap[0][0] <= now + 1e-6:
            tag = heapq.heappop(heap)[2]
            if tag is not None:
                came[tag] = now
                for link, new, links in follow(tag):
                    count += 1
                    heapq.heappush(waiting[link], (-left(new), count, new, links, now))
        for link, line in waiting.items():
            if line and free[link] <= now + 1e-6:
                _, _, new, links, since = heapq.heappop(line)
                free[link] = now + links * 0.655
                starts.append((max(since, now - AHEAD), now, link, new))
                count += 2
                heapq.heappush(heap, (free[link], count - 1, None))
                heapq.heappush(heap, (free[link] + 2.2 + 0.6 * links, count, new))
    order = [(tag, []) for tag in came]
    times = list(came.values())
    for issue, _, link, new in sorted(starts, key=lambda x: x[1]):
        order[sum(t <= issue + 1e-6 for t in times) - 1][1].append((link, new))
    return order


ORDER = plan()
CUTS = (10, 10, 8, 4)


def filled(tag):
    kind = tag[0]
    if kind == "own":
        return [(0, 0, 0), (1, 0, 0)]
    if kind == "Ay":
        return [(0, 0, tag[2])] if tag[1] == "s" else []
    if kind == "Az":
        return [(0, tag[2], tag[1])]
    if kind == "Bz":
        return [(1, tag[1], 0)]
    return [(1, tag[2], 2 if kind == "Bo" else 3 if tag[1] == "+" else 1)]


COME = [[b[1:] for tag, _ in ORDER for b in filled(tag) if b[0] == half] for half in (0, 1)]
STARTS = [sum(CUTS[:i]) for i in range(len(CUTS))]
TAGS = [tag for tag, _ in ORDER[1:]]
TAGS += [(k, r) for k in ("h", "f") for r in range(1, NT)]
TAGS += [(k, r) for k in ("y1", "ty") for r in range(1, NY)]
TAGS += [(k, r) for k in ("z1", "tz") for r in range(1, NZ)]
TAGS += [("pu",), ("pd",)] + [("c",)] + [("p", i, r) for i in range(3) for r in range(8) if i or r]
INDEX = {tag: i for i, tag in enumerate(TAGS)}


def kernel(
    act_in, cot_in, lengths_in, down_in, up_in, proj_in, target_in, out,
    act, cot, lengths, down, up, proj, target, pc, neighbours, own_blocks, other, ga, gb, hid, hrecv, facs, total, twin, rounded, precv,
    tqz, along, zsum, lsem, ssem, rsem,
):
    dp, me = lax.axis_index("dp"), lax.axis_index("tensor")
    z, y = lax.div(dp, NY), lax.rem(dp, NY)
    parity = lax.rem(z, 2)

    def at_z(o):
        return lax.rem(z + (o % NZ), NZ)

    def at_y(o):
        return lax.rem(y + (o % NY), NY)

    def at_t(o):
        return lax.rem(me + (o % NT), NT)

    def dev(zz, yy):
        return (zz * NY + yy, me)

    def copy(tag, src, dst, device):
        i = INDEX[tag]
        return pltpu.make_async_remote_copy(
            src_ref=src, dst_ref=dst, send_sem=ssem.at[i], recv_sem=rsem.at[i],
            device_id=device, device_id_type=MESH,
        )

    sent = []

    def send(tag, src, dst, device):
        c = copy(tag, src, dst, device)
        c.start()
        sent.append(c)

    def settle(some):
        for c in sent[:some]:
            c.wait_send()
        del sent[:some]

    def wait(tag, ref):
        copy(tag, ref, ref, dev(at_z(1), y)).wait_recv()

    here_y = pl.ds(pl.multiple_of(y * 128, 128), 128)
    ends = (
        (down_in, down), (act_in, act), (up_in, up), (cot_in, cot),
        (target_in, target.at[:, here_y]), (lengths_in, lengths), (proj_in, proj),
    )
    loads = [pltpu.make_async_copy(a, b, lsem.at[i]) for i, (a, b) in enumerate(ends)]
    for c in loads:
        c.start()

    barrier = pltpu.get_barrier_semaphore()
    partners = [(dp, at_t(r)) for r in range(1, NT)]
    partners += [dev(at_z(o), y) for o in range(1, NZ)] + [dev(z, at_y(o)) for o in range(1, NY)]
    partners += [(at_z(o) * NY + y, at_t(r)) for o in (-1, 1) for r in range(2, NT, 2)]
    for p in partners:
        pl.semaphore_signal(barrier, inc=1, device_id=p, device_id_type=MESH)

    nt = (((1,), (1,)), ((), ()))
    loads[0].wait()
    loads[1].wait()
    for e in range(8):
        hid[8 + e] = lax.dot_general(down[...], act[e], nt, preferred_element_type=F32)
    loads[2].wait()
    loads[3].wait()
    for e in range(8):
        hid[e] = lax.dot_general(up[...], cot[e], nt, preferred_element_type=F32)
    pl.semaphore_wait(barrier, len(partners))
    loads[6].wait()
    theirs = pl.multiple_of((1 - parity) * 4096, 4096)
    for r in range(1, NT):
        p = at_t(r)
        send(("h", r), hid.at[p], hrecv.at[me], (dp, p))
    send(("pu",), proj.at[pl.ds(theirs, 2048)], neighbours.at[0], dev(at_z(-1), y))
    send(("pd",), proj.at[pl.ds(theirs + 2048, 2048)], neighbours.at[1], dev(at_z(1), y))
    hrecv[me] = hid[me]

    loads[4].wait()
    for r in range(1, NY):
        send(("ty", r), target.at[:, here_y], target.at[:, here_y], dev(z, at_y(r)))

    q = lax.broadcasted_iota(jnp.int32, (256, 256), 0)
    c = lax.broadcasted_iota(jnp.int32, (256, 256), 1)
    swap = jnp.where(c == lax.rem(q, 16) * 16 + lax.div(q, 16), 1.0, 0.0).astype(BF16)

    def turn(source, first, to):
        def step(b, carry):
            block = source[pl.ds(pl.multiple_of(first + b * 256, 256), 256), :]
            moved = jnp.dot(swap, block, preferred_element_type=F32).astype(BF16)
            for j in range(16):
                at = pl.ds(pl.multiple_of(b * 16 + (j % 8) * 128, 16), 16)
                to[at, (j // 8) * 128 : (j // 8) * 128 + 128] = moved[j * 16 : j * 16 + 16]
            return carry

        lax.fori_loop(0, 8, step, 0, unroll=True)

    mine = pl.multiple_of(parity * 4096, 4096)
    turn(proj, mine, pc.at[0])

    for r in range(1, NT):
        wait(("h", r), hrecv.at[at_t(-r)])
    hidden = hrecv[0]
    for t in range(1, NT):
        hidden = hidden + hrecv[t]
    loads[5].wait()
    token = lax.broadcasted_iota(jnp.int32, (8, 128), 1)
    facs[me] = jnp.where(token < lengths[lax.rem(me, 8)], SCALE, 0.0) * hidden
    for r in range(1, NT):
        send(("f", r), facs.at[me], facs.at[me], (dp, at_t(r)))

    settle(NT - 1)
    turn(proj, mine + 2048, pc.at[1])
    total[...] = jnp.zeros((2, 3, 8, 2, 8, 128), F32)

    for r in range(1, NT):
        wait(("f", r), facs.at[at_t(-r)])
    own = lax.broadcasted_iota(jnp.int32, (8, 8, 128), 1)
    grads = []
    for a, data in ((0, act), (1, cot)):
        parts = []
        for e in range(8):
            spread = jnp.broadcast_to(facs[a * 8 + e][:, None, :], (8, 8, 128))
            parts.append(jnp.where(own == e, spread, 0.0).reshape(64, 128).astype(BF16))
        left = jnp.concatenate(parts, axis=1)
        grads.append(jnp.dot(left, data[...].reshape(1024, 512), preferred_element_type=F32))
    for j in range(8):
        tile = jnp.concatenate([g[j * 8 : j * 8 + 8] for g in grads], axis=0).astype(BF16)
        for i in range(4):
            own_blocks[i, :, j * 128 : j * 128 + 128] = tile[:, i * 128 : i * 128 + 128]
    same, not_same = 2 * parity, 2 - 2 * parity
    ga[dp] = own_blocks[same]
    gb[y * NZ + z] = own_blocks[same + 1]

    def slot_index_a(o, r):
        return at_z(o) * NY + at_y(r)

    def slot_index_b(o, r):
        return at_y(r) * NZ + at_z(o)

    def slot_a(o, r):
        return ga.at[slot_index_a(o, r)]

    def slot_b(o, r):
        return gb.at[slot_index_b(o, r)]

    def slot(tag):
        kind = tag[0]
        if kind == "Ay":
            return slot_a(0, tag[2]) if tag[1] == "s" else other.at[tag[2] - 1]
        if kind == "Az":
            return slot_a(tag[2], tag[1])
        if kind == "Bz":
            return slot_b(tag[1], 0)
        return slot_b(tag[2], 2 if kind == "Bo" else 3 if tag[1] == "+" else 1)

    def ends_of(link, new):
        kind = new[0]
        s = 1 if link[1] == "+" else -1
        if kind == "Ay":
            _, c, r = new
            if c == "s":
                ref = slot_a(0, 0 if r != 2 else -s)
                return ref, ref
            here = own_blocks.at[not_same] if r != 2 else other.at[(-s) % NY - 1]
            return here, other.at[r - 1]
        if kind in ("Az", "Bz"):
            o, r = new[-1], new[1] if kind == "Az" else 0
            place = slot_a if kind == "Az" else slot_b
            if abs(o) == 1:
                there = place(0, r)
                if kind == "Bz":
                    return own_blocks.at[not_same + 1], there
                return (own_blocks.at[not_same] if r == 0 else other.at[r - 1]), there
            ref = place(0 if abs(o) == 2 else -s * (abs(o) - 2), r)
            return ref, ref
        ref = slot_b(new[2], 0 if kind == "By" else -s)
        return ref, ref

    def fold(found):
        found = found.reshape(-1, 2, 8, 256)
        return found[:, 0, :, :128] + found[:, 1, :, 128:]

    def product(half, first, count):
        gathered, slots = ((ga, slot_index_a), (gb, slot_index_b))[half]
        places = COME[half][first : first + count]
        block = jnp.concatenate([gathered[slots(o, r)] for o, r in places], axis=0)
        mine = fold(jnp.dot(block, pc[half], preferred_element_type=F32))
        next_one = fold(jnp.dot(block, pc[2 + half], preferred_element_type=F32))
        for i, (o, r) in enumerate(places):
            core_of, pair = lax.div(at_y(r), 2), lax.rem(at_y(r), 2)
            total[core_of, 0, at_z(o), pair] += mine[i]
            total[core_of, 1 + half, at_z(o), pair] = next_one[i]

    def validation():
        for r in range(1, NY):
            lanes = pl.ds(pl.multiple_of(at_y(-r) * 128, 128), 128)
            wait(("ty", r), target.at[:, lanes])
        ones = jnp.ones((8, 512), F32)
        wide = target[...].astype(F32)
        tqz[z] = lax.dot_general(
            ones, wide * wide, nt, precision=lax.Precision.HIGHEST, preferred_element_type=F32
        )
        for r in range(1, NZ):
            send(("tz", r), tqz.at[z], tqz.at[z], dev(at_z(r), y))

    seen = [0, 0]
    for tag, sends in ORDER:
        if tag != ("own",):
            wait(tag, slot(tag))
        for link, new in sends:
            links = 1 if link[0] == "y" or abs(new[-1]) == 1 else 2
            step = links if link[1] == "+" else -links
            to = dev(at_z(step), y) if link[0] == "z" else dev(z, at_y(step))
            send(new, *ends_of(link, new), to)
        for half, _, _ in filled(tag):
            seen[half] += 1
            for first, count in zip(STARTS, CUTS):
                if seen[half] == first + count:
                    if first == 0:
                        wait(("pd",) if half else ("pu",), neighbours.at[half])
                        turn(neighbours.at[half], 0, pc.at[2 + half])
                    product(half, first, count)

    core, spot = lax.rem(me, 2), lax.div(me, 2)
    send(("c",), total.at[1 - core], twin, (dp, me + 1 - 2 * core))
    wait(("c",), twin)
    for i, o in ((1, 1), (2, -1), (0, 0)):
        both_cores = total[core, i] + twin[i]
        rounded[i] = both_cores.reshape(8, 16, 128).astype(BF16)
        for r in range(8):
            if i or r:
                q = lax.rem(spot + r, 8)
                to = (at_z(o) * NY + y, q * 2 + core)
                send(("p", i, r), rounded.at[i, q], precv.at[i, spot], to)
    validation()
    settle(len(sent) - NZ + 1)
    precv[0, spot] = rounded[0, spot]
    projected = jnp.zeros((16, 128), F32)
    for i in (1, 2, 0):
        for r in range(8):
            if i or r:
                wait(("p", i, r), precv.at[i, lax.rem(spot + 8 - r, 8)])
    for i in range(3):
        for t in range(8):
            projected = projected + precv[i, t].astype(F32)
    along[y] = projected
    for r in range(1, NY):
        send(("y1", r), along.at[y], along.at[y], dev(z, at_y(r)))
    for r in range(1, NY):
        wait(("y1", r), along.at[at_y(-r)])
    wide = jnp.concatenate([along[i] for i in range(NY)], axis=1)
    high = wide.astype(BF16)
    rest = wide - high.astype(F32)
    middle = rest.astype(BF16)
    low = (rest - middle.astype(F32)).astype(BF16)
    three = lax.dot_general(
        jnp.concatenate([high, middle, low], axis=0), target[...], nt, preferred_element_type=F32
    )
    zsum[z, :, :256] = ((three[32:] + three[16:32]) + three[:16]).astype(BF16)
    square = jnp.sum(wide * wide, axis=1, keepdims=True)
    zsum[z, :, 256:] = jnp.broadcast_to(square, (16, 128)).astype(BF16)
    for r in range(1, NZ):
        send(("z1", r), zsum.at[z], zsum.at[z], dev(at_z(r), y))
    settle(len(sent) - NZ + 1)
    for r in range(1, NZ):
        wait(("tz", r), tqz.at[at_z(-r)])
    norm = tqz[0]
    for t in range(1, NZ):
        norm = norm + tqz[t]
    norm = math.sqrt(K) * lax.rsqrt(norm[0:1] + EPS)
    for r in range(1, NZ):
        wait(("z1", r), zsum.at[at_z(-r)])
    both = zsum[0].astype(F32)
    for t in range(1, NZ):
        both = both + zsum[t].astype(F32)
    own_norm = lax.rsqrt(both[:, 256:] + EPS)
    out[:, :128] = both[:, :128] * own_norm * norm[:, :128]
    out[:, 128:] = both[:, 128:256] * own_norm * norm[:, 128:]
    settle(len(sent))


def body(activations, cotangents, lengths, down, up, projection, target):
    vmem, hbm = pl.BlockSpec(memory_space=pltpu.VMEM), pl.BlockSpec(memory_space=pl.ANY)
    return pl.pallas_call(
        kernel,
        out_shape=jax.ShapeDtypeStruct((16, 256), F32),
        in_specs=[hbm] * 7,
        out_specs=vmem,
        scratch_shapes=[
            pltpu.VMEM((8, 128, 512), BF16),
            pltpu.VMEM((8, 128, 512), BF16),
            pltpu.SMEM((8,), jnp.int32),
            pltpu.VMEM((8, 512), BF16),
            pltpu.VMEM((8, 512), BF16),
            pltpu.VMEM((8192, 128), BF16),
            pltpu.VMEM((256, 512), BF16),
            pltpu.VMEM((4, W, 256), BF16),
            pltpu.VMEM((2, 2048, 128), BF16),
            pltpu.VMEM((4, 16, W), BF16),
            pltpu.VMEM((3, 16, W), BF16),
            pltpu.VMEM((32, 16, W), BF16),
            pltpu.VMEM((32, 16, W), BF16),
            pltpu.VMEM((16, 8, 128), F32),
            pltpu.VMEM((16, 8, 128), F32),
            pltpu.VMEM((16, 8, 128), F32),
            pltpu.VMEM((2, 3, 8, 2, 8, 128), F32),
            pltpu.VMEM((3, 8, 2, 8, 128), F32),
            pltpu.VMEM((3, 8, 16, 128), BF16),
            pltpu.VMEM((3, 8, 16, 128), BF16),
            pltpu.VMEM((8, 8, 256), F32),
            pltpu.VMEM((4, 16, 128), F32),
            pltpu.VMEM((8, 16, 384), BF16),
            pltpu.SemaphoreType.DMA((7,)),
            pltpu.SemaphoreType.DMA((len(TAGS),)),
            pltpu.SemaphoreType.DMA((len(TAGS),)),
        ],
        compiler_params=pltpu.CompilerParams(
            collective_id=0, has_side_effects=True, vmem_limit_bytes=60 * 1024 * 1024
        ),
    )(activations, cotangents, lengths, down.T, up, projection, target)


def solution(mesh):
    placed = (
        P("dp", None, "tensor"),
        P("dp", None, "tensor"),
        P("dp"),
        P("tensor", None),
        P(None, "tensor"),
        P("tensor", "dp"),
        P(None, "dp"),
    )
    return jax.shard_map(
        body, mesh=mesh, in_specs=placed, out_specs=P("tensor", None), check_vma=False
    )
```
